256 devices in a mesh: ctx: 32 (over x, y, core), grp: 8 (over z).
Axes of the slice: x: 4, y: 4, z: 8, core: 2. Of those that a mesh axis runs over, the one named last changes fastest.
Arguments:
- tokens: bfloat16 [8, 20480, 768], P('grp', 'ctx'), may hold values from -48 to 48
- slot_query: bfloat16 [768, 1024], replicated, may hold values from -0.4330127 to 0.4330127
- expert_in: bfloat16 [256, 768, 3072], P(('ctx', 'grp')), may hold values from -1.796875 to 1.796875
- expert_out: bfloat16 [256, 3072, 768], P(('ctx', 'grp')), may hold values from -0.47851562 to 0.47851562
Outputs:
- mixed: bfloat16 [8, 20480, 768], P('grp', 'ctx')
The draws below stay inside these ranges and needn't reach their ends.
All inputs are finite; a program needn't handle non-finite values.
Results may differ from the reference program's by a relative error of at most 0.015.
Values may be sent and summed in bfloat16 or wider, within the bound.
No kernel may reach another device: no remote copies, remote signals or barrier semaphores. Data moves between devices by JAX's collectives and lax.ppermute only.
A program may use at most 64 MiB of HBM per device.

```python
import math
import jax
import jax.numpy as jnp
from jax import lax

D = 768
H = 3072
P_SIZE = 4
EXPERTS = 256
SLOTS = 1024
LENGTH = 20480
SEQS = 8


def query_base(key):
    normal_part = jax.random.normal(jax.random.fold_in(key, 11), (D, SLOTS), jnp.float32)
    base = jnp.clip(normal_part, -6.0, 6.0) * (2.0 / math.sqrt(D))
    lower_rows = (jnp.arange(D) < D // 2)[:, None]
    first_columns = (jnp.arange(SLOTS) < 32)[None, :]
    return jnp.where(lower_rows == first_columns, base, 0.02 * base)


def draw_slot_query(key, part):
    base = query_base(key)
    return base.astype(jnp.bfloat16)


def draw_tokens(key, part):
    base = query_base(key)
    key = jax.random.fold_in(key, 3)
    values = jnp.clip(jax.random.normal(key, (SEQS, LENGTH, D), jnp.float32), -6.0, 6.0)
    lower = (jnp.arange(D) < D // 2).astype(jnp.float32)
    upper = 1.0 - lower
    own_noise = jnp.clip(values, -4.0, 4.0) * upper[None, None, :]
    block_length = max(LENGTH // 16, 2)
    position = jnp.arange(LENGTH)
    block_index = jnp.minimum(position // block_length, 15)
    within = position % block_length
    column = 2 * (block_index % 32)
    unit = 1.0 / (0.8 * math.sqrt(D))
    level = 120.0 + 60.0 * (block_index % 5).astype(jnp.float32)
    leading = within < 2
    second_half = jnp.logical_and(within >= block_length // 2, block_index % 4 == 1)
    second_half = jnp.logical_and(second_half, jnp.logical_not(leading))
    target = jnp.where(leading, level - 2.0 * within.astype(jnp.float32), level - 7.5)
    noise_scale = jnp.where(leading, 3.0, 0.5)
    strength = target * unit
    signs = jnp.sign(base)[:, column].T * lower[None, :]
    block_noise = jnp.clip(jax.random.normal(jax.random.fold_in(key, 9), (SEQS, 16, D), jnp.float32), -4.0, 4.0) * lower[None, None, :]
    aligned = strength[None, :, None] * signs[None, :, :] + block_noise[:, block_index, :] + noise_scale[None, :, None] * own_noise
    aligned = jnp.clip(aligned, -48.0, 48.0)
    chosen = jnp.logical_or(leading, second_half)
    values = jnp.where(chosen[None, :, None], aligned, values)
    return values.astype(jnp.bfloat16)


def steps_of(stream_key, shape, cuts, least, high):
    factor_of, own = 1.0, jax.random.fold_in(stream_key, 6)
    for dim, blocks in cuts:
        steps = jnp.exp(jax.random.uniform(jax.random.fold_in(own, dim), (blocks,), jnp.float32, least / len(cuts), high / len(cuts)))
        factor_of = factor_of * jnp.repeat(steps, shape[dim] // blocks).reshape([-1 if axis == dim else 1 for axis in range(len(shape))])
    return factor_of


def centred(rng, shape, width, limit, cuts=(), dtype=jnp.bfloat16):
    entries = jax.random.normal(rng, shape, jnp.float32) * width
    if len(cuts) > 0:
        entries = steps_of(rng, shape, cuts, -0.22, 0.18) * entries
    return jnp.clip(entries, min=-limit, max=limit).astype(dtype)


def setup_inputs(seed: int = 0) -> dict:
    splits = jax.random.split(jax.random.key(seed), 5)
    return {
        "tokens": draw_tokens(jax.random.fold_in(splits[4], 71), 0),
        "slot_query": draw_slot_query(jax.random.fold_in(splits[4], 71), 0),
        "expert_in": centred(splits[2], (EXPERTS, D, H), 0.3, 1.796875, ((0, 256),)),
        "expert_out": centred(splits[3], (EXPERTS, H, D), 0.08, 0.47851562, ((0, 256),)),
    }


def sequence_logits(tokens_one, slot_query):
    return jnp.dot(tokens_one, slot_query, preferred_element_type=jnp.float32)


def dispatch_one(tokens_one, slot_query):
    logits = sequence_logits(tokens_one, slot_query)
    column_max = jnp.max(logits, axis=0, keepdims=True)
    scaled = jnp.exp(logits - column_max)
    dispatch = (scaled / jnp.sum(scaled, axis=0, keepdims=True)).astype(jnp.bfloat16)
    return jnp.dot(dispatch.T, tokens_one, preferred_element_type=jnp.float32).astype(jnp.bfloat16)


def expert_mlp(operands):
    slot_rows, weight_in, weight_out = operands
    hidden = jax.nn.gelu(jnp.dot(slot_rows, weight_in, preferred_element_type=jnp.float32), approximate=True).astype(jnp.bfloat16)
    return jnp.dot(hidden, weight_out, preferred_element_type=jnp.float32).astype(jnp.bfloat16)


def reference(tokens, slot_query, expert_in, expert_out):
    slot_inputs = lax.map(lambda tokens_one: dispatch_one(tokens_one, slot_query), tokens)
    grouped = slot_inputs.reshape(SEQS, EXPERTS, P_SIZE, D).transpose(1, 0, 2, 3).reshape(EXPERTS, SEQS * P_SIZE, D)
    outputs = lax.map(expert_mlp, (grouped, expert_in, expert_out))
    slot_outputs = outputs.reshape(EXPERTS, SEQS, P_SIZE, D).transpose(1, 0, 2, 3).reshape(SEQS, SLOTS, D)

    def combine_one(operands):
        tokens_one, outputs_one = operands
        logits = sequence_logits(tokens_one, slot_query)
        row_max = jnp.max(logits, axis=1, keepdims=True)
        scaled = jnp.exp(logits - row_max)
        combine = (scaled / jnp.sum(scaled, axis=1, keepdims=True)).astype(jnp.bfloat16)
        return jnp.dot(combine, outputs_one, preferred_element_type=jnp.float32).astype(jnp.bfloat16)

    return lax.map(combine_one, (tokens, slot_outputs))
```

```python
import jax
import jax.numpy as jnp
from jax import lax
from jax.sharding import Mesh, PartitionSpec as P

BF16 = jnp.bfloat16
F32 = jnp.float32
SWAP = [(0, 1), (1, 0)]


def pack(sums, peak, total):
    high = lax.reduce_precision(total, 8, 7)
    extra = jnp.stack([peak, high, total - high], axis=1)
    extra = jnp.pad(extra, ((0, 0), (0, 125)))
    return jnp.concatenate([sums.astype(BF16), extra.astype(BF16)], axis=1)


def unpack(rows, width):
    sums = rows[..., :width].astype(F32)
    extra = rows[..., width:width + 3].astype(F32)
    return sums, extra[..., 0], extra[..., 1] + extra[..., 2]


def partial_sums(local_tokens, query):
    logits = jnp.dot(local_tokens, query, preferred_element_type=F32)
    peak = lax.reduce_precision(jnp.max(logits, axis=0), 8, 7)
    scaled = jnp.exp(logits - peak[None, :])
    sums = lax.dot_general(
        scaled.astype(BF16), local_tokens, (((0,), (0,)), ((), ())), preferred_element_type=F32
    )
    return logits, sums, peak, jnp.sum(scaled, axis=0)


def per_device(tokens, slot_query, expert_in, expert_out):
    local_tokens = tokens[0]
    width = local_tokens.shape[1]
    chips = lax.axis_size("x") * lax.axis_size("y")
    grp_count = lax.axis_size("grp")
    slots = slot_query.shape[1]
    slot_rows = slots // (2 * chips)
    core = lax.axis_index("core")
    split = slot_query.reshape(width, chips, 2, slot_rows)
    first = split[:, :, 0].reshape(width, slots // 2)
    second = split[:, :, 1].reshape(width, slots // 2)
    own_query = jnp.where(core == 0, first, second)
    other_query = jnp.where(core == 0, second, first)

    other_logits, sums, peak, total = partial_sums(local_tokens, other_query)
    arrived = lax.ppermute(pack(sums, peak, total), "core", SWAP)
    own_logits, sums, peak, total = partial_sums(local_tokens, own_query)
    sums2, peak2, total2 = unpack(arrived, width)
    top = jnp.maximum(peak, peak2)
    w1, w2 = jnp.exp(peak - top), jnp.exp(peak2 - top)
    sums = sums * w1[:, None] + sums2 * w2[:, None]
    packed = pack(sums, top, total * w1 + total2 * w2)
    parts = lax.all_to_all(
        packed.reshape(chips, slot_rows, -1), ("x", "y"), split_axis=0, concat_axis=0, tiled=True
    )
    sums, peak, total = unpack(parts, width)
    weight = jnp.exp(peak - jnp.max(peak, axis=0))
    slot_inputs = (
        jnp.sum(sums * weight[..., None], axis=0) / jnp.sum(total * weight, axis=0)[:, None]
    ).astype(BF16)

    received = lax.all_to_all(
        slot_inputs.reshape(grp_count, slot_rows // grp_count, width),
        "grp", split_axis=0, concat_axis=0, tiled=True,
    )
    hidden = jax.nn.gelu(
        jnp.dot(received.reshape(-1, width), expert_in[0], preferred_element_type=F32),
        approximate=True,
    ).astype(BF16)
    produced = jnp.dot(hidden, expert_out[0], preferred_element_type=F32).astype(BF16)
    returned = lax.all_to_all(
        produced.reshape(received.shape), "grp", split_axis=0, concat_axis=0, tiled=True
    ).reshape(1, slot_rows, width)
    own = lax.all_to_all(
        jnp.broadcast_to(returned, (chips, slot_rows, width)),
        ("x", "y"), split_axis=0, concat_axis=0, tiled=True,
    ).reshape(slots // 2, width)
    other = lax.ppermute(own, "core", SWAP)

    row_max = jnp.maximum(jnp.max(own_logits, axis=1), jnp.max(other_logits, axis=1))[:, None]
    own_weights = jnp.exp(own_logits - row_max)
    other_weights = jnp.exp(other_logits - row_max)
    row_total = jnp.sum(own_weights, axis=1) + jnp.sum(other_weights, axis=1)
    mixed = jnp.dot(own_weights.astype(BF16), own, preferred_element_type=F32)
    mixed = mixed + jnp.dot(other_weights.astype(BF16), other, preferred_element_type=F32)
    return (mixed / row_total[:, None]).astype(BF16)[None]


def solution(mesh):
    fine = Mesh(mesh.devices.reshape(4, 4, 2, 8), ("x", "y", "core", "grp"))
    ctx = ("x", "y", "core")
    in_specs = (
        P("grp", ctx, None),
        P(),
        P(ctx + ("grp",), None, None),
        P(ctx + ("grp",), None, None),
    )
    return jax.shard_map(
        per_device, mesh=fine, in_specs=in_specs, out_specs=P("grp", ctx, None), check_vma=False
    )
```

```python
import jax
import jax.numpy as jnp
from jax import lax
from jax.experimental import pallas as pl
from jax.experimental.pallas import tpu as pltpu
from jax.sharding import Mesh, PartitionSpec as P

BF16 = jnp.bfloat16
F32 = jnp.float32
SWAP = [(0, 1), (1, 0)]
LIMIT = 24 * 1024 * 1024
EXTRA = 128
TRANSPOSED = (((1,), (1,)), ((), ()))


def dot(a, b, dims=(((1,), (0,)), ((), ()))):
    return lax.dot_general(a, b, dims, preferred_element_type=F32)


def call(body, outs, flops, moved, *args):
    return pl.pallas_call(
        body,
        out_shape=outs,
        in_specs=[pl.BlockSpec(memory_space=pltpu.VMEM)] * len(args),
        out_specs=[pl.BlockSpec(memory_space=pltpu.VMEM)] * len(outs),
        compiler_params=pltpu.CompilerParams(vmem_limit_bytes=LIMIT),
        cost_estimate=pl.CostEstimate(flops=flops, bytes_accessed=moved, transcendentals=0),
    )(*args)


def row_kernel(own_q, other_q, x, own_logits, own_w, other_w):
    tokens = x[...]
    own = dot(own_q[...], tokens, TRANSPOSED)
    other = dot(other_q[...], tokens, TRANSPOSED)
    own_logits[...] = own
    top = jnp.maximum(jnp.max(own, axis=0, keepdims=True), jnp.max(other, axis=0, keepdims=True))
    own = jnp.exp(own - top)
    other = jnp.exp(other - top)
    total = jnp.sum(own, axis=0, keepdims=True) + jnp.sum(other, axis=0, keepdims=True)
    scale = 1.0 / total
    own_w[...] = (own * scale).astype(BF16)
    other_w[...] = (other * scale).astype(BF16)


def column_kernel(own_q, logits, x, x2, out):
    slots, width = own_q.shape
    block = 128
    lane = lax.broadcasted_iota(jnp.int32, (block, EXTRA), 1)
    for start in range(0, slots, block):
        rows = slice(start, start + block)
        first = logits[rows, :]
        second = dot(own_q[rows, :], x2[...], TRANSPOSED)
        top = jnp.maximum(
            jnp.max(first, axis=1, keepdims=True), jnp.max(second, axis=1, keepdims=True)
        )
        top = top.astype(BF16).astype(F32)
        first = jnp.exp(first - top)
        second = jnp.exp(second - top)
        total = jnp.sum(first, axis=1, keepdims=True) + jnp.sum(second, axis=1, keepdims=True)
        high = total.astype(BF16).astype(F32)
        sums = dot(first.astype(BF16), x[...]) + dot(second.astype(BF16), x2[...])
        out[rows, :width] = sums.astype(BF16)
        extra = jnp.where(lane == 0, top, jnp.where(lane == 1, high, total - high))
        out[rows, width:] = extra.astype(BF16)


def expert_kernel(rows, w_in, w_out, out):
    hidden = w_in.shape[1]
    step = 768
    x = rows[...]
    acc = jnp.zeros(out.shape, F32)
    for start in range(0, hidden, step):
        part = slice(start, start + step)
        h = jax.nn.gelu(dot(x, w_in[:, part]), approximate=True).astype(BF16)
        acc = acc + dot(h, w_out[part, :])
    out[...] = acc.astype(BF16)


def unpack(rows, width):
    sums = rows[..., :width].astype(F32)
    extra = rows[..., width : width + 3].astype(F32)
    return sums, extra[..., 0], extra[..., 1] + extra[..., 2]


def per_device(tokens, slot_query, expert_in, expert_out):
    x = tokens[0]
    count, width = x.shape
    chips = lax.axis_size("x") * lax.axis_size("y")
    grp_count = lax.axis_size("grp")
    slots = slot_query.shape[1]
    half = slots // 2
    slot_rows = half // chips
    x2 = lax.ppermute(x, "core", SWAP)

    core = lax.axis_index("core")
    split = slot_query.T.reshape(chips, 2, slot_rows, width)
    own_q = jnp.where(core == 0, split[:, 0], split[:, 1]).reshape(half, width)
    other_q = jnp.where(core == 0, split[:, 1], split[:, 0]).reshape(half, width)
    own_logits, own_w, other_w = call(
        row_kernel,
        [
            jax.ShapeDtypeStruct((half, count), F32),
            jax.ShapeDtypeStruct((half, count), BF16),
            jax.ShapeDtypeStruct((half, count), BF16),
        ],
        2 * slots * width * count, 5_000_000, own_q, other_q, x,
    )
    (packed,) = call(
        column_kernel,
        [jax.ShapeDtypeStruct((half, width + EXTRA), BF16)],
        3 * slots * width * count, 5_000_000, own_q, own_logits, x, x2,
    )
    parts = lax.all_to_all(
        packed.reshape(chips, slot_rows, -1), ("x", "y"), split_axis=0, concat_axis=0, tiled=True
    )
    sums, peak, total = unpack(parts, width)
    weight = jnp.exp(peak - jnp.max(peak, axis=0))
    slot_inputs = (
        jnp.sum(sums * weight[..., None], axis=0) / jnp.sum(total * weight, axis=0)[:, None]
    ).astype(BF16)

    received = lax.all_to_all(
        slot_inputs.reshape(grp_count, slot_rows // grp_count, width),
        "grp", split_axis=0, concat_axis=0, tiled=True,
    )
    (produced,) = call(
        expert_kernel,
        [jax.ShapeDtypeStruct((slot_rows, width), BF16)],
        4 * slot_rows * width * expert_in.shape[2], 9_500_000,
        received.reshape(slot_rows, width),
        pltpu.with_memory_space_constraint(expert_in[0], pltpu.VMEM),
        pltpu.with_memory_space_constraint(expert_out[0], pltpu.VMEM),
    )
    returned = lax.all_to_all(
        produced.reshape(received.shape), "grp", split_axis=0, concat_axis=0, tiled=True
    ).reshape(1, slot_rows, width)
    own = lax.all_to_all(
        jnp.broadcast_to(returned, (chips, slot_rows, width)),
        ("x", "y"), split_axis=0, concat_axis=0, tiled=True,
    ).reshape(half, width)
    other = lax.ppermute(own, "core", SWAP)
    over_slots = (((0,), (0,)), ((), ()))
    mixed = dot(own_w, own, over_slots)
    mixed = mixed + dot(other_w, other, over_slots)
    return mixed.astype(BF16)[None]


def solution(mesh):
    fine = Mesh(mesh.devices.reshape(4, 4, 2, 8), ("x", "y", "core", "grp"))
    ctx = ("x", "y", "core")
    in_specs = (
        P("grp", ctx, None),
        P(),
        P(ctx + ("grp",), None, None),
        P(ctx + ("grp",), None, None),
    )
    return jax.shard_map(
        per_device, mesh=fine, in_specs=in_specs, out_specs=P("grp", ctx, None), check_vma=False
    )
```

```python
import functools

import jax
import jax.numpy as jnp
from jax import lax
from jax.experimental import pallas as pl
from jax.experimental.pallas import tpu as pltpu
from jax.sharding import Mesh, PartitionSpec as P

BF16 = jnp.bfloat16
F32 = jnp.float32
SWAP = [(0, 1), (1, 0)]
LIMIT = 24 * 1024 * 1024
FRONT = LIMIT
BLOCK = 512
EXTRA = 128
TRANSPOSED = (((1,), (1,)), ((), ()))


def dot(a, b, dims=(((1,), (0,)), ((), ()))):
    return lax.dot_general(a, b, dims, preferred_element_type=F32)


def call(body, outs, flops, moved, args, scratch=(), space=pltpu.VMEM, limit=LIMIT):
    return pl.pallas_call(
        body,
        out_shape=outs,
        in_specs=[pl.BlockSpec(memory_space=space)] * len(args),
        out_specs=[pl.BlockSpec(memory_space=pltpu.VMEM)] * len(outs),
        scratch_shapes=list(scratch),
        compiler_params=pltpu.CompilerParams(vmem_limit_bytes=limit),
        cost_estimate=pl.CostEstimate(flops=flops, bytes_accessed=moved, transcendentals=0),
    )(*args)


def peak_of(logits):
    return jnp.max(logits, axis=1, keepdims=True).astype(BF16).astype(F32)


def row_kernel(slot_rows, q_hbm, x_hbm, own_q, own_logits, other_logits, sums, stats, q, x, other_q, sems):
    group = 256
    kept = group // 2
    blocks = q.shape[1] // group
    loads = []
    for b in range(blocks):
        columns = slice(b * group, (b + 1) * group)
        loads.append(
            pltpu.make_async_copy(q_hbm.at[:, columns], q.at[:, columns], sems.at[b])
        )
    loads.append(pltpu.make_async_copy(x_hbm, x, sems.at[blocks]))
    for load in loads:
        load.start()
    core = lax.axis_index("core")
    pair = 2 * slot_rows
    row = lax.broadcasted_iota(jnp.int32, (group, group), 0)
    column = lax.broadcasted_iota(jnp.int32, (group, group), 1)
    kind = row // kept
    row = row % kept
    place = row // slot_rows * pair + row % slot_rows + (kind ^ core) * slot_rows
    pick = jnp.where(column == place, 1.0, 0.0).astype(BF16)
    for b in range(blocks):
        loads[b].wait()
        picked = dot(pick, q[:, b * group : (b + 1) * group], TRANSPOSED).astype(BF16)
        rows = slice(b * kept, (b + 1) * kept)
        own_q[rows, :] = picked[:kept]
        other_q[rows, :] = picked[kept:]
    loads[blocks].wait()
    tokens = x[...]
    own = [dot(own_q[rows, :], tokens, TRANSPOSED) for rows in halves(own_q)]
    lane = lax.broadcasted_iota(jnp.int32, (BLOCK, EXTRA), 1)
    for rows, logits in zip(halves(own_q), own):
        own_logits[rows, :] = logits
        top = peak_of(logits)
        scaled = jnp.exp(logits - top)
        total = jnp.sum(scaled, axis=1, keepdims=True)
        sums[rows, :] = dot(scaled.astype(BF16), tokens)
        stats[rows, :] = jnp.where(lane == 0, top, total)
        other_logits[rows, :] = dot(other_q[rows, :], tokens, TRANSPOSED)


def halves(ref):
    return [slice(start, start + BLOCK) for start in range(0, ref.shape[0], BLOCK)]


def softmax_kernel(own_logits, other_logits, own_w, other_w):
    own, other = own_logits[...], other_logits[...]
    top = jnp.maximum(jnp.max(own, axis=0, keepdims=True), jnp.max(other, axis=0, keepdims=True))
    own = jnp.exp(own - top)
    other = jnp.exp(other - top)
    total = jnp.sum(own, axis=0, keepdims=True) + jnp.sum(other, axis=0, keepdims=True)
    scale = 1.0 / total
    own_w[...] = (own * scale).astype(BF16)
    other_w[...] = (other * scale).astype(BF16)


def column_kernel(own_q, x2, sums, stats, out):
    width = own_q.shape[1]
    tokens = x2[...]
    lane = lax.broadcasted_iota(jnp.int32, (BLOCK, EXTRA), 1)
    parts = [dot(own_q[rows, :], tokens, TRANSPOSED) for rows in halves(own_q)]
    for rows, logits in zip(halves(own_q), parts):
        top2 = peak_of(logits)
        scaled = jnp.exp(logits - top2)
        top1, total1 = stats[rows, 0:1], stats[rows, 1:2]
        top = jnp.maximum(top1, top2)
        w1, w2 = jnp.exp(top1 - top), jnp.exp(top2 - top)
        total = total1 * w1 + jnp.sum(scaled, axis=1, keepdims=True) * w2
        both = sums[rows, :] * w1 + dot(scaled.astype(BF16), tokens) * w2
        out[rows, :width] = both.astype(BF16)
        high = total.astype(BF16).astype(F32)
        extra = jnp.where(lane == 0, top, jnp.where(lane == 1, high, total - high))
        out[rows, width:] = extra.astype(BF16)


def combine_kernel(parts, out, scratch):
    chips = parts.shape[0]
    groups, held, width = out.shape
    extra = [parts[c, :, width:].astype(F32) for c in range(chips)]
    top = extra[0][:, 0:1]
    for c in range(1, chips):
        top = jnp.maximum(top, extra[c][:, 0:1])
    total = jnp.zeros(top.shape, F32)
    acc = jnp.zeros(scratch.shape, F32)
    for c in range(chips):
        weight = jnp.exp(extra[c][:, 0:1] - top)
        total = total + weight * (extra[c][:, 1:2] + extra[c][:, 2:3])
        acc = acc + weight * parts[c, :, :width].astype(F32)
    scratch[...] = acc / total
    for g in range(groups):
        out[g] = scratch[g * held : (g + 1) * held, :].astype(BF16)


def expert_kernel(received, w_in, w_out, out, scratch):
    groups, held, _ = received.shape
    for g in range(groups):
        scratch[g * held : (g + 1) * held, :] = received[g].astype(F32)
    x = scratch[...].astype(BF16)
    hidden = w_in.shape[1]
    step = 768
    acc = jnp.zeros(scratch.shape, F32)
    for start in range(0, hidden, step):
        part = slice(start, start + step)
        h = jax.nn.gelu(dot(x, w_in[:, part]), approximate=True).astype(BF16)
        acc = acc + dot(h, w_out[part, :])
    scratch[...] = acc
    for g in range(groups):
        out[g] = scratch[g * held : (g + 1) * held, :].astype(BF16)


def per_device(tokens, slot_query, expert_in, expert_out):
    x = tokens[0]
    count, width = x.shape
    chips = lax.axis_size("x") * lax.axis_size("y")
    grp_count = lax.axis_size("grp")
    slots = slot_query.shape[1]
    half = slots // 2
    slot_rows = half // chips
    x2 = lax.ppermute(x, "core", SWAP)
    shape = jax.ShapeDtypeStruct
    own_q, own_logits, other_logits, sums, stats = call(
        functools.partial(row_kernel, slot_rows),
        [
            shape((half, width), BF16),
            shape((half, count), F32),
            shape((half, count), F32),
            shape((half, width), F32),
            shape((half, EXTRA), F32),
        ],
        3 * slots * width * count, 5_000_000,
        [pltpu.with_memory_space_constraint(a, pltpu.HBM) for a in (slot_query, x)],
        [
            pltpu.VMEM((width, slots), BF16),
            pltpu.VMEM((count, width), BF16),
            pltpu.VMEM((half, width), BF16),
            pltpu.SemaphoreType.DMA((5,)),
        ],
        pl.ANY,
        FRONT,
    )
    (packed,) = call(
        column_kernel,
        [shape((half, width + EXTRA), BF16)],
        2 * slots * width * count, 5_000_000, (own_q, x2, sums, stats), limit=FRONT,
    )
    w_in, w_out = expert_in[0], expert_out[0]
    parts = lax.all_to_all(
        packed.reshape(chips, slot_rows, -1), ("x", "y"), split_axis=0, concat_axis=0, tiled=True
    )
    block = shape((grp_count, slot_rows // grp_count, width), BF16)
    rows = [pltpu.VMEM((slot_rows, width), F32)]
    (slot_inputs,) = call(combine_kernel, [block], 2 * half * width, 1_000_000, (parts,), rows)
    received = lax.all_to_all(slot_inputs, "grp", split_axis=0, concat_axis=0, tiled=True)
    (produced,) = call(
        expert_kernel,
        [block],
        4 * slot_rows * width * expert_in.shape[2], 9_500_000,
        (
            received,
            pltpu.with_memory_space_constraint(w_in, pltpu.VMEM),
            pltpu.with_memory_space_constraint(w_out, pltpu.VMEM),
        ),
        rows,
    )
    returned = lax.all_to_all(
        produced, "grp", split_axis=0, concat_axis=0, tiled=True
    ).reshape(1, slot_rows, width)
    own = lax.all_to_all(
        jnp.broadcast_to(returned, (chips, slot_rows, width)),
        ("x", "y"), split_axis=0, concat_axis=0, tiled=True,
    ).reshape(half, width)
    other = lax.ppermute(own, "core", SWAP)
    own_w, other_w = call(
        softmax_kernel,
        [shape((half, count), BF16), shape((half, count), BF16)],
        10 * slots * count, 4_000_000, (own_logits, other_logits),
    )
    over_slots = (((0,), (0,)), ((), ()))
    mixed = dot(own_w, own, over_slots)
    mixed = mixed + dot(other_w, other, over_slots)
    return mixed.astype(BF16)[None]


def solution(mesh):
    fine = Mesh(mesh.devices.reshape(4, 4, 2, 8), ("x", "y", "core", "grp"))
    ctx = ("x", "y", "core")
    in_specs = (
        P("grp", ctx, None),
        P(),
        P(ctx + ("grp",), None, None),
        P(ctx + ("grp",), None, None),
    )
    return jax.shard_map(
        per_device, mesh=fine, in_specs=in_specs, out_specs=P("grp", ctx, None), check_vma=False
    )
```

```python
import functools

import jax
import jax.numpy as jnp
from jax import lax
from jax.experimental import pallas as pl
from jax.experimental.pallas import tpu as pltpu
from jax.sharding import Mesh, PartitionSpec as P

BF16 = jnp.bfloat16
F32 = jnp.float32
SWAP = [(0, 1), (1, 0)]
LIMIT = 24 * 1024 * 1024
LANES = 128
TAIL = 16
OVER_ROWS = (((0,), (0,)), ((), ()))


def dot(a, b, dims=(((1,), (0,)), ((), ()))):
    return lax.dot_general(a, b, dims, preferred_element_type=F32)


def call(body, outs, flops, moved, args, scratch=(), space=pltpu.VMEM):
    return pl.pallas_call(
        body,
        out_shape=outs,
        in_specs=[pl.BlockSpec(memory_space=space)] * len(args),
        out_specs=[pl.BlockSpec(memory_space=pltpu.VMEM)] * len(outs),
        scratch_shapes=list(scratch),
        compiler_params=pltpu.CompilerParams(vmem_limit_bytes=LIMIT),
        cost_estimate=pl.CostEstimate(flops=flops, bytes_accessed=moved, transcendentals=0),
    )(*args)


def peak_of(logits):
    return jnp.max(logits, axis=0, keepdims=True).astype(BF16).astype(F32)


def logit_kernel(slot_rows, q_hbm, x_hbm, own_q, other_q, x, logits, q, sems):
    group = 256
    kept = group // 2
    blocks = q.shape[1] // group
    loads = []
    for b in range(blocks):
        columns = slice(b * group, (b + 1) * group)
        loads.append(
            pltpu.make_async_copy(q_hbm.at[:, columns], q.at[:, columns], sems.at[b])
        )
    loads.append(pltpu.make_async_copy(x_hbm, x, sems.at[blocks]))
    for load in loads:
        load.start()
    core = lax.axis_index("core")
    pair = 2 * slot_rows
    row = lax.broadcasted_iota(jnp.int32, (group, group), 0)
    column = lax.broadcasted_iota(jnp.int32, (group, group), 1)
    kind = column // kept
    column = column % kept
    place = column // slot_rows * pair + column % slot_rows + (kind ^ core) * slot_rows
    pick = jnp.where(row == place, 1.0, 0.0).astype(BF16)
    for b in range(blocks):
        loads[b].wait()
        picked = dot(q[:, b * group : (b + 1) * group], pick).astype(BF16)
        columns = slice(b * kept, (b + 1) * kept)
        own_q[:, columns] = picked[:, :kept]
        other_q[:, columns] = picked[:, kept:]
    loads[blocks].wait()
    logits[...] = dot(x[...], own_q[...])


def column_kernel(own_q, x, x2, logits, out):
    width = own_q.shape[0]
    second = dot(x2[...], own_q[...])
    first = logits[...]
    top1 = peak_of(first)
    first = jnp.exp(first - top1)
    total1 = jnp.sum(first, axis=0, keepdims=True)
    sums1 = dot(first.astype(BF16), x[...], OVER_ROWS)
    top2 = peak_of(second)
    second = jnp.exp(second - top2)
    total2 = jnp.sum(second, axis=0, keepdims=True)
    sums2 = dot(second.astype(BF16), x2[...], OVER_ROWS)
    top = jnp.maximum(top1, top2)
    w1, w2 = jnp.exp(top1 - top), jnp.exp(top2 - top)
    total = total1 * w1 + total2 * w2
    high = total.astype(BF16).astype(F32)
    kind = lax.broadcasted_iota(jnp.int32, (LANES, top.shape[1]), 0)
    stats = total - high
    for place, value in enumerate((top, high, w1, w2)):
        stats = jnp.where(kind == place, value, stats)
    columns = stats.T
    sums = (sums1 * columns[:, 2:3] + sums2 * columns[:, 3:4]).astype(BF16)
    stats = stats[:TAIL].astype(BF16)
    chips, rows, _ = out.shape
    held = top.shape[1] // chips
    for c in range(chips):
        for j in range(width // LANES):
            part = slice(j * LANES, (j + 1) * LANES)
            out[c, j * held : (j + 1) * held, :] = sums[c * held : (c + 1) * held, part]
        group = c * held // LANES * LANES
        out[c, rows - TAIL :, :] = stats[:, group : group + LANES]


def softmax_kernel(x, other_q, logits, own_w, other_w):
    own = logits[...]
    other = dot(x[...], other_q[...])
    top = jnp.maximum(jnp.max(own, axis=1, keepdims=True), jnp.max(other, axis=1, keepdims=True))
    own = jnp.exp(own - top)
    other = jnp.exp(other - top)
    total = jnp.sum(own, axis=1, keepdims=True) + jnp.sum(other, axis=1, keepdims=True)
    scale = 1.0 / total
    own_w[...] = (own * scale).astype(BF16)
    other_w[...] = (other * scale).astype(BF16)


def combine_kernel(parts, out, weights, scratch):
    chips, rows, _ = parts.shape
    groups, size, width = out.shape
    held = groups * size
    source = lax.broadcasted_iota(jnp.int32, (LANES, LANES), 0)
    top = jnp.full((LANES, LANES), -jnp.inf, F32)
    total = jnp.zeros((LANES, LANES), F32)
    for c in range(chips):
        stats = parts[c, rows - TAIL :, :].astype(F32)
        top = jnp.where(source == c, stats[0:1], top)
        total = jnp.where(source == c, stats[1:2] + stats[4:5], total)
    weight = jnp.exp(top - jnp.max(top, axis=0, keepdims=True))
    weight = weight / jnp.sum(total * weight, axis=0, keepdims=True)
    weights[...] = weight.T
    chip = lax.axis_index("x") * lax.axis_size("y") + lax.axis_index("y")
    start = pl.multiple_of(chip % (LANES // held) * held, held)
    mine = weights[pl.ds(start, held), :]
    for j in range(width // LANES):
        part = slice(j * LANES, (j + 1) * LANES)
        acc = jnp.zeros((held, LANES), F32)
        for c in range(chips):
            acc = acc + mine[:, c : c + 1] * parts[c, j * held : (j + 1) * held, :].astype(F32)
        scratch[:, part] = acc
    for g in range(groups):
        out[g] = scratch[g * size : (g + 1) * size, :].astype(BF16)


def expert_kernel(received, w_in, w_out, out, scratch):
    groups, held, _ = received.shape
    for g in range(groups):
        scratch[g * held : (g + 1) * held, :] = received[g].astype(F32)
    x = scratch[...].astype(BF16)
    hidden = w_in.shape[1]
    step = 768
    acc = jnp.zeros(scratch.shape, F32)
    for start in range(0, hidden, step):
        part = slice(start, start + step)
        h = jax.nn.gelu(dot(x, w_in[:, part]), approximate=True).astype(BF16)
        acc = acc + dot(h, w_out[part, :])
    scratch[...] = acc
    for g in range(groups):
        out[g] = scratch[g * held : (g + 1) * held, :].astype(BF16)


def per_device(tokens, slot_query, expert_in, expert_out):
    x = tokens[0]
    count, width = x.shape
    chips = lax.axis_size("x") * lax.axis_size("y")
    grp_count = lax.axis_size("grp")
    slots = slot_query.shape[1]
    half = slots // 2
    slot_rows = half // chips
    x2 = lax.ppermute(x, "core", SWAP)
    shape = jax.ShapeDtypeStruct
    own_q, other_q, kept, logits = call(
        functools.partial(logit_kernel, slot_rows),
        [
            shape((width, half), BF16),
            shape((width, half), BF16),
            shape((count, width), BF16),
            shape((count, half), F32),
        ],
        2 * slots * width * count, 5_000_000,
        [pltpu.with_memory_space_constraint(a, pltpu.HBM) for a in (slot_query, x)],
        [pltpu.VMEM((width, slots), BF16), pltpu.SemaphoreType.DMA((5,))],
        pl.ANY,
    )
    (packed,) = call(
        column_kernel,
        [shape((chips, slot_rows * width // LANES + TAIL, LANES), BF16)],
        3 * slots * width * count, 5_000_000, (own_q, kept, x2, logits),
    )
    w_in, w_out = expert_in[0], expert_out[0]
    parts = lax.all_to_all(
        packed, ("x", "y"), split_axis=0, concat_axis=0, tiled=True
    )
    block = shape((grp_count, slot_rows // grp_count, width), BF16)
    rows = [pltpu.VMEM((slot_rows, width), F32)]
    (slot_inputs,) = call(
        combine_kernel, [block], 2 * half * width, 1_000_000, (parts,),
        [pltpu.VMEM((LANES, LANES), F32)] + rows,
    )
    received = lax.all_to_all(slot_inputs, "grp", split_axis=0, concat_axis=0, tiled=True)
    (produced,) = call(
        expert_kernel,
        [block],
        4 * slot_rows * width * expert_in.shape[2], 9_500_000,
        (
            received,
            pltpu.with_memory_space_constraint(w_in, pltpu.VMEM),
            pltpu.with_memory_space_constraint(w_out, pltpu.VMEM),
        ),
        rows,
    )
    returned = lax.all_to_all(
        produced, "grp", split_axis=0, concat_axis=0, tiled=True
    ).reshape(1, slot_rows, width)
    own = lax.all_to_all(
        jnp.broadcast_to(returned, (chips, slot_rows, width)),
        ("x", "y"), split_axis=0, concat_axis=0, tiled=True,
    ).reshape(half, width)
    other = lax.ppermute(own, "core", SWAP)
    own_w, other_w = call(
        softmax_kernel,
        [shape((count, half), BF16), shape((count, half), BF16)],
        slots * width * count, 4_000_000, (kept, other_q, logits),
    )
    mixed = dot(own_w, own) + dot(other_w, other)
    return mixed.astype(BF16)[None]


def solution(mesh):
    fine = Mesh(mesh.devices.reshape(4, 4, 2, 8), ("x", "y", "core", "grp"))
    ctx = ("x", "y", "core")
    in_specs = (
        P("grp", ctx, None),
        P(),
        P(ctx + ("grp",), None, None),
        P(ctx + ("grp",), None, None),
    )
    return jax.shard_map(
        per_device, mesh=fine, in_specs=in_specs, out_specs=P("grp", ctx, None), check_vma=False
    )
```

```python
import functools

import jax
import jax.numpy as jnp
from jax import lax
from jax.experimental import pallas as pl
from jax.experimental.pallas import tpu as pltpu
from jax.sharding import Mesh, PartitionSpec as P

BF16 = jnp.bfloat16
F32 = jnp.float32
SWAP = [(0, 1), (1, 0)]
LIMIT = 24 * 1024 * 1024
LANES = 128
TAIL = 16
CHUNKS = 2
OVER_ROWS = (((0,), (0,)), ((), ()))


def dot(a, b, dims=(((1,), (0,)), ((), ()))):
    return lax.dot_general(a, b, dims, preferred_element_type=F32)


def call(body, outs, flops, moved, args, scratch=(), space=pltpu.VMEM):
    return pl.pallas_call(
        body,
        out_shape=outs,
        in_specs=[pl.BlockSpec(memory_space=space)] * len(args),
        out_specs=[pl.BlockSpec(memory_space=pltpu.VMEM)] * len(outs),
        scratch_shapes=list(scratch),
        compiler_params=pltpu.CompilerParams(vmem_limit_bytes=LIMIT),
        cost_estimate=pl.CostEstimate(flops=flops, bytes_accessed=moved, transcendentals=0),
    )(*args)


def peak_of(logits):
    return jnp.max(logits, axis=0, keepdims=True).astype(BF16).astype(F32)


def logit_kernel(slot_rows, q_hbm, x_hbm, own_q, other_q, x, logits, q, sems):
    group = 256
    kept = group // 2
    chunk = q.shape[0] // CHUNKS
    chunks = [slice(i * chunk, (i + 1) * chunk) for i in range(CHUNKS)]
    loads = [
        pltpu.make_async_copy(q_hbm.at[rows, :], q.at[rows, :], sems.at[i])
        for i, rows in enumerate(chunks)
    ]
    loads.append(pltpu.make_async_copy(x_hbm, x, sems.at[CHUNKS]))
    for load in loads:
        load.start()
    core = lax.axis_index("core")
    pair = 2 * slot_rows
    row = lax.broadcasted_iota(jnp.int32, (group, group), 0)
    column = lax.broadcasted_iota(jnp.int32, (group, group), 1)
    kind = column // kept
    column = column % kept
    place = column // slot_rows * pair + column % slot_rows + (kind ^ core) * slot_rows
    pick = jnp.where(row == place, 1.0, 0.0).astype(BF16)
    for load, rows in zip(loads, chunks):
        load.wait()
        for b in range(q.shape[1] // group):
            picked = dot(q[rows, b * group : (b + 1) * group], pick).astype(BF16)
            columns = slice(b * kept, (b + 1) * kept)
            own_q[rows, columns] = picked[:, :kept]
            other_q[rows, columns] = picked[:, kept:]
    loads[CHUNKS].wait()
    logits[...] = dot(x[...], own_q[...])


def column_kernel(own_q, x, x2, logits, out):
    width = own_q.shape[0]
    second = dot(x2[...], own_q[...])
    first = logits[...]
    top1 = peak_of(first)
    first = jnp.exp(first - top1)
    total1 = jnp.sum(first, axis=0, keepdims=True)
    sums1 = dot(first.astype(BF16), x[...], OVER_ROWS)
    top2 = peak_of(second)
    second = jnp.exp(second - top2)
    total2 = jnp.sum(second, axis=0, keepdims=True)
    sums2 = dot(second.astype(BF16), x2[...], OVER_ROWS)
    top = jnp.maximum(top1, top2)
    w1, w2 = jnp.exp(top1 - top), jnp.exp(top2 - top)
    total = total1 * w1 + total2 * w2
    high = total.astype(BF16).astype(F32)
    kind = lax.broadcasted_iota(jnp.int32, (LANES, top.shape[1]), 0)
    stats = total - high
    for place, value in enumerate((top, high, w1, w2)):
        stats = jnp.where(kind == place, value, stats)
    columns = stats.T
    sums = (sums1 * columns[:, 2:3] + sums2 * columns[:, 3:4]).astype(BF16)
    stats = stats[:TAIL].astype(BF16)
    chips, rows, _ = out.shape
    held = top.shape[1] // chips
    for c in range(chips):
        for j in range(width // LANES):
            part = slice(j * LANES, (j + 1) * LANES)
            out[c, j * held : (j + 1) * held, :] = sums[c * held : (c + 1) * held, part]
        group = c * held // LANES * LANES
        out[c, rows - TAIL :, :] = stats[:, group : group + LANES]


def softmax_kernel(x, other_q, logits, own_w, other_w):
    own = logits[...]
    other = dot(x[...], other_q[...])
    top = jnp.maximum(jnp.max(own, axis=1, keepdims=True), jnp.max(other, axis=1, keepdims=True))
    own = jnp.exp(own - top)
    other = jnp.exp(other - top)
    total = jnp.sum(own, axis=1, keepdims=True) + jnp.sum(other, axis=1, keepdims=True)
    scale = 1.0 / total
    own_w[...] = (own * scale).astype(BF16)
    other_w[...] = (other * scale).astype(BF16)


def combine_kernel(parts, out, weights, scratch):
    chips, rows, _ = parts.shape
    groups, size, width = out.shape
    held = groups * size
    source = lax.broadcasted_iota(jnp.int32, (LANES, LANES), 0)
    top = jnp.full((LANES, LANES), -jnp.inf, F32)
    total = jnp.zeros((LANES, LANES), F32)
    for c in range(chips):
        stats = parts[c, rows - TAIL :, :].astype(F32)
        top = jnp.where(source == c, stats[0:1], top)
        total = jnp.where(source == c, stats[1:2] + stats[4:5], total)
    weight = jnp.exp(top - jnp.max(top, axis=0, keepdims=True))
    weight = weight / jnp.sum(total * weight, axis=0, keepdims=True)
    weights[...] = weight.T
    chip = lax.axis_index("x") * lax.axis_size("y") + lax.axis_index("y")
    start = pl.multiple_of(chip % (LANES // held) * held, held)
    mine = weights[pl.ds(start, held), :]
    for j in range(width // LANES):
        part = slice(j * LANES, (j + 1) * LANES)
        acc = jnp.zeros((held, LANES), F32)
        for c in range(chips):
            acc = acc + mine[:, c : c + 1] * parts[c, j * held : (j + 1) * held, :].astype(F32)
        scratch[:, part] = acc
    for g in range(groups):
        out[g] = scratch[g * size : (g + 1) * size, :].astype(BF16)


def expert_kernel(received, w_in, w_out, out, scratch):
    groups, held, _ = received.shape
    for g in range(groups):
        scratch[g * held : (g + 1) * held, :] = received[g].astype(F32)
    x = scratch[...].astype(BF16)
    h = jax.nn.gelu(dot(x, w_in[...]), approximate=True).astype(BF16)
    scratch[...] = dot(h, w_out[...])
    for g in range(groups):
        out[g] = scratch[g * held : (g + 1) * held, :].astype(BF16)


def per_device(tokens, slot_query, expert_in, expert_out):
    x = tokens[0]
    count, width = x.shape
    chips = lax.axis_size("x") * lax.axis_size("y")
    grp_count = lax.axis_size("grp")
    slots = slot_query.shape[1]
    half = slots // 2
    slot_rows = half // chips
    x2 = lax.ppermute(x, "core", SWAP)
    shape = jax.ShapeDtypeStruct
    own_q, other_q, kept, logits = call(
        functools.partial(logit_kernel, slot_rows),
        [
            shape((width, half), BF16),
            shape((width, half), BF16),
            shape((count, width), BF16),
            shape((count, half), F32),
        ],
        2 * slots * width * count, 5_000_000,
        [pltpu.with_memory_space_constraint(a, pltpu.HBM) for a in (slot_query, x)],
        [pltpu.VMEM((width, slots), BF16), pltpu.SemaphoreType.DMA((CHUNKS + 1,))],
        pl.ANY,
    )
    (packed,) = call(
        column_kernel,
        [shape((chips, slot_rows * width // LANES + TAIL, LANES), BF16)],
        3 * slots * width * count, 5_000_000, (own_q, kept, x2, logits),
    )
    w_in, w_out = expert_in[0], expert_out[0]
    parts = lax.all_to_all(
        packed, ("x", "y"), split_axis=0, concat_axis=0, tiled=True
    )
    block = shape((grp_count, slot_rows // grp_count, width), BF16)
    rows = [pltpu.VMEM((slot_rows, width), F32)]
    (slot_inputs,) = call(
        combine_kernel, [block], 2 * half * width, 1_000_000, (parts,),
        [pltpu.VMEM((LANES, LANES), F32)] + rows,
    )
    received = lax.all_to_all(slot_inputs, "grp", split_axis=0, concat_axis=0, tiled=True)
    (produced,) = call(
        expert_kernel,
        [block],
        4 * slot_rows * width * expert_in.shape[2], 9_500_000,
        (
            received,
            pltpu.with_memory_space_constraint(w_in, pltpu.VMEM),
            pltpu.with_memory_space_constraint(w_out, pltpu.VMEM),
        ),
        rows,
    )
    returned = lax.all_to_all(
        produced, "grp", split_axis=0, concat_axis=0, tiled=True
    ).reshape(1, slot_rows, width)
    own = lax.all_to_all(
        jnp.broadcast_to(returned, (chips, slot_rows, width)),
        ("x", "y"), split_axis=0, concat_axis=0, tiled=True,
    ).reshape(half, width)
    other = lax.ppermute(own, "core", SWAP)
    own_w, other_w = call(
        softmax_kernel,
        [shape((count, half), BF16), shape((count, half), BF16)],
        slots * width * count, 4_000_000, (kept, other_q, logits),
    )
    mixed = dot(own_w, own) + dot(other_w, other)
    return mixed.astype(BF16)[None]


def solution(mesh):
    fine = Mesh(mesh.devices.reshape(4, 4, 2, 8), ("x", "y", "core", "grp"))
    ctx = ("x", "y", "core")
    in_specs = (
        P("grp", ctx, None),
        P(),
        P(ctx + ("grp",), None, None),
        P(ctx + ("grp",), None, None),
    )
    return jax.shard_map(
        per_device, mesh=fine, in_specs=in_specs, out_specs=P("grp", ctx, None), check_vma=False
    )
```

```python
import functools

import jax
import jax.numpy as jnp
from jax import lax
from jax.experimental import pallas as pl
from jax.experimental.pallas import tpu as pltpu
from jax.sharding import Mesh, PartitionSpec as P

BF16 = jnp.bfloat16
F32 = jnp.float32
SWAP = [(0, 1), (1, 0)]
LIMIT = 24 * 1024 * 1024
LANES = 128
TAIL = 16
CHUNKS = 2
PIECES = 4
OVER_ROWS = (((0,), (0,)), ((), ()))


def dot(a, b, dims=(((1,), (0,)), ((), ()))):
    return lax.dot_general(a, b, dims, preferred_element_type=F32)


def call(body, outs, flops, moved, args, scratch=(), space=pltpu.VMEM, to=pltpu.VMEM):
    return pl.pallas_call(
        body,
        out_shape=outs,
        in_specs=[pl.BlockSpec(memory_space=space)] * len(args),
        out_specs=[pl.BlockSpec(memory_space=to)] * len(outs),
        scratch_shapes=list(scratch),
        compiler_params=pltpu.CompilerParams(vmem_limit_bytes=LIMIT),
        cost_estimate=pl.CostEstimate(flops=flops, bytes_accessed=moved, transcendentals=0),
    )(*args)


def peak_of(logits):
    return jnp.max(logits, axis=0, keepdims=True).astype(BF16).astype(F32)


def logit_kernel(slot_rows, q_hbm, x_hbm, own_q, other_q, x, logits, q, sems):
    group = 256
    kept = group // 2
    chunk = q.shape[0] // CHUNKS
    chunks = [slice(i * chunk, (i + 1) * chunk) for i in range(CHUNKS)]
    loads = [
        pltpu.make_async_copy(q_hbm.at[rows, :], q.at[rows, :], sems.at[i])
        for i, rows in enumerate(chunks)
    ]
    loads.append(pltpu.make_async_copy(x_hbm, x, sems.at[CHUNKS]))
    for load in loads:
        load.start()
    core = lax.axis_index("core")
    pair = 2 * slot_rows
    row = lax.broadcasted_iota(jnp.int32, (group, group), 0)
    column = lax.broadcasted_iota(jnp.int32, (group, group), 1)
    kind = column // kept
    column = column % kept
    place = column // slot_rows * pair + column % slot_rows + (kind ^ core) * slot_rows
    pick = jnp.where(row == place, 1.0, 0.0).astype(BF16)
    for load, rows in zip(loads, chunks):
        load.wait()
        for b in range(q.shape[1] // group):
            picked = dot(q[rows, b * group : (b + 1) * group], pick).astype(BF16)
            columns = slice(b * kept, (b + 1) * kept)
            own_q[rows, columns] = picked[:, :kept]
            other_q[rows, columns] = picked[:, kept:]
    loads[CHUNKS].wait()
    logits[...] = dot(x[...], own_q[...])


def column_kernel(own_q, x, x2, logits, out):
    width = own_q.shape[0]
    second = dot(x2[...], own_q[...])
    first = logits[...]
    top1 = peak_of(first)
    first = jnp.exp(first - top1)
    total1 = jnp.sum(first, axis=0, keepdims=True)
    sums1 = dot(first.astype(BF16), x[...], OVER_ROWS)
    top2 = peak_of(second)
    second = jnp.exp(second - top2)
    total2 = jnp.sum(second, axis=0, keepdims=True)
    sums2 = dot(second.astype(BF16), x2[...], OVER_ROWS)
    top = jnp.maximum(top1, top2)
    w1, w2 = jnp.exp(top1 - top), jnp.exp(top2 - top)
    total = total1 * w1 + total2 * w2
    high = total.astype(BF16).astype(F32)
    kind = lax.broadcasted_iota(jnp.int32, (LANES, top.shape[1]), 0)
    stats = total - high
    for place, value in enumerate((top, high, w1, w2)):
        stats = jnp.where(kind == place, value, stats)
    columns = stats.T
    sums = (sums1 * columns[:, 2:3] + sums2 * columns[:, 3:4]).astype(BF16)
    stats = stats[:TAIL].astype(BF16)
    chips, rows, _ = out.shape
    held = top.shape[1] // chips
    for c in range(chips):
        for j in range(width // LANES):
            part = slice(j * LANES, (j + 1) * LANES)
            out[c, j * held : (j + 1) * held, :] = sums[c * held : (c + 1) * held, part]
        group = c * held // LANES * LANES
        out[c, rows - TAIL :, :] = stats[:, group : group + LANES]


def softmax_kernel(x, other_q, logits, own_w, other_w):
    own = logits[...]
    other = dot(x[...], other_q[...])
    top = jnp.maximum(jnp.max(own, axis=1, keepdims=True), jnp.max(other, axis=1, keepdims=True))
    own = jnp.exp(own - top)
    other = jnp.exp(other - top)
    total = jnp.sum(own, axis=1, keepdims=True) + jnp.sum(other, axis=1, keepdims=True)
    scale = 1.0 / total
    own_w[...] = (own * scale).astype(BF16)
    other_w[...] = (other * scale).astype(BF16)


def combine_kernel(parts, out, weights, scratch):
    chips, rows, _ = parts.shape
    groups, size, width = out.shape
    held = groups * size
    source = lax.broadcasted_iota(jnp.int32, (LANES, LANES), 0)
    top = jnp.full((LANES, LANES), -jnp.inf, F32)
    total = jnp.zeros((LANES, LANES), F32)
    for c in range(chips):
        stats = parts[c, rows - TAIL :, :].astype(F32)
        top = jnp.where(source == c, stats[0:1], top)
        total = jnp.where(source == c, stats[1:2] + stats[4:5], total)
    weight = jnp.exp(top - jnp.max(top, axis=0, keepdims=True))
    weight = weight / jnp.sum(total * weight, axis=0, keepdims=True)
    weights[...] = weight.T
    chip = lax.axis_index("x") * lax.axis_size("y") + lax.axis_index("y")
    start = pl.multiple_of(chip % (LANES // held) * held, held)
    mine = weights[pl.ds(start, held), :]
    for j in range(width // LANES):
        part = slice(j * LANES, (j + 1) * LANES)
        acc = jnp.zeros((held, LANES), F32)
        for c in range(chips):
            acc = acc + mine[:, c : c + 1] * parts[c, j * held : (j + 1) * held, :].astype(F32)
        scratch[:, part] = acc
    for g in range(groups):
        out[g] = scratch[g * size : (g + 1) * size, :].astype(BF16)


def expert_kernel(received, w_in, w_out, out, scratch):
    groups, held, _ = received.shape
    for g in range(groups):
        scratch[g * held : (g + 1) * held, :] = received[g].astype(F32)
    x = scratch[...].astype(BF16)
    h = jax.nn.gelu(dot(x, w_in[...]), approximate=True).astype(BF16)
    scratch[...] = dot(h, w_out[...])
    for g in range(groups):
        out[g] = scratch[g * held : (g + 1) * held, :].astype(BF16)


def final_kernel(partial, weights, rows, out, buffer, sems):
    count = buffer.shape[0] // PIECES
    stores = []
    for i in range(PIECES):
        part = slice(i * count, (i + 1) * count)
        buffer[part, :] = (partial[part, :] + dot(weights[part, :], rows[...])).astype(BF16)
        stores.append(pltpu.make_async_copy(buffer.at[part, :], out.at[part, :], sems.at[i]))
        stores[i].start()
    for store in stores:
        store.wait()


def per_device(tokens, slot_query, expert_in, expert_out):
    x = tokens[0]
    count, width = x.shape
    chips = lax.axis_size("x") * lax.axis_size("y")
    grp_count = lax.axis_size("grp")
    slots = slot_query.shape[1]
    half = slots // 2
    slot_rows = half // chips
    x2 = lax.ppermute(x, "core", SWAP)
    shape = jax.ShapeDtypeStruct
    own_q, other_q, kept, logits = call(
        functools.partial(logit_kernel, slot_rows),
        [
            shape((width, half), BF16),
            shape((width, half), BF16),
            shape((count, width), BF16),
            shape((count, half), F32),
        ],
        2 * slots * width * count, 5_000_000,
        [pltpu.with_memory_space_constraint(a, pltpu.HBM) for a in (slot_query, x)],
        [pltpu.VMEM((width, slots), BF16), pltpu.SemaphoreType.DMA((CHUNKS + 1,))],
        pl.ANY,
    )
    (packed,) = call(
        column_kernel,
        [shape((chips, slot_rows * width // LANES + TAIL, LANES), BF16)],
        3 * slots * width * count, 5_000_000, (own_q, kept, x2, logits),
    )
    w_in, w_out = expert_in[0], expert_out[0]
    parts = lax.all_to_all(
        packed, ("x", "y"), split_axis=0, concat_axis=0, tiled=True
    )
    block = shape((grp_count, slot_rows // grp_count, width), BF16)
    rows = [pltpu.VMEM((slot_rows, width), F32)]
    (slot_inputs,) = call(
        combine_kernel, [block], 2 * half * width, 1_000_000, (parts,),
        [pltpu.VMEM((LANES, LANES), F32)] + rows,
    )
    received = lax.all_to_all(slot_inputs, "grp", split_axis=0, concat_axis=0, tiled=True)
    (produced,) = call(
        expert_kernel,
        [block],
        4 * slot_rows * width * expert_in.shape[2], 9_500_000,
        (
            received,
            pltpu.with_memory_space_constraint(w_in, pltpu.VMEM),
            pltpu.with_memory_space_constraint(w_out, pltpu.VMEM),
        ),
        rows,
    )
    returned = lax.all_to_all(
        produced, "grp", split_axis=0, concat_axis=0, tiled=True
    ).reshape(1, slot_rows, width)
    own = lax.all_to_all(
        jnp.broadcast_to(returned, (chips, slot_rows, width)),
        ("x", "y"), split_axis=0, concat_axis=0, tiled=True,
    ).reshape(half, width)
    other = lax.ppermute(own, "core", SWAP)
    own_w, other_w = call(
        softmax_kernel,
        [shape((count, half), BF16), shape((count, half), BF16)],
        slots * width * count, 4_000_000, (kept, other_q, logits),
    )
    (mixed,) = call(
        final_kernel,
        [shape((count, width), BF16)],
        slots * width * count, 4_000_000, (dot(own_w, own), other_w, other),
        [pltpu.VMEM((count, width), BF16), pltpu.SemaphoreType.DMA((PIECES,))],
        to=pl.ANY,
    )
    return mixed[None]


def solution(mesh):
    fine = Mesh(mesh.devices.reshape(4, 4, 2, 8), ("x", "y", "core", "grp"))
    ctx = ("x", "y", "core")
    in_specs = (
        P("grp", ctx, None),
        P(),
        P(ctx + ("grp",), None, None),
        P(ctx + ("grp",), None, None),
    )
    return jax.shard_map(
        per_device, mesh=fine, in_specs=in_specs, out_specs=P("grp", ctx, None), check_vma=False
    )
```

```python
import functools

import jax
import jax.numpy as jnp
from jax import lax
from jax.experimental import pallas as pl
from jax.experimental.pallas import tpu as pltpu
from jax.sharding import Mesh, PartitionSpec as P

BF16 = jnp.bfloat16
F32 = jnp.float32
SWAP = [(0, 1), (1, 0)]
CTX = ("x", "y", "core")
LIMIT = 24 * 1024 * 1024
LANES = 128
TAIL = 16
CHUNKS = 2
PIECES = 4
TURN_X, TURN_Y, TURN_Z = 2, 2, 4
OVER_ROWS = (((0,), (0,)), ((), ()))


def dot(a, b, dims=(((1,), (0,)), ((), ()))):
    return lax.dot_general(a, b, dims, preferred_element_type=F32)


def call(body, outs, flops, moved, args, scratch=(), space=pltpu.VMEM, to=pltpu.VMEM):
    return pl.pallas_call(
        body,
        out_shape=outs,
        in_specs=[pl.BlockSpec(memory_space=space)] * len(args),
        out_specs=[pl.BlockSpec(memory_space=to)] * len(outs),
        scratch_shapes=list(scratch),
        compiler_params=pltpu.CompilerParams(vmem_limit_bytes=LIMIT),
        cost_estimate=pl.CostEstimate(flops=flops, bytes_accessed=moved, transcendentals=0),
    )(*args)


def peak_of(logits):
    return jnp.max(logits, axis=0, keepdims=True).astype(BF16).astype(F32)


def logit_kernel(slot_rows, turn, q_hbm, x_hbm, own_q, other_q, x, logits, q, sems):
    group = 256
    kept = group // 2
    chunk = q.shape[0] // CHUNKS
    chunks = [slice(i * chunk, (i + 1) * chunk) for i in range(CHUNKS)]
    loads = [
        pltpu.make_async_copy(q_hbm.at[rows, :], q.at[rows, :], sems.at[i])
        for i, rows in enumerate(chunks)
    ]
    loads.append(pltpu.make_async_copy(x_hbm, x, sems.at[CHUNKS]))
    for load in loads:
        load.start()
    core = lax.axis_index("core")
    pair = 2 * slot_rows
    row = lax.broadcasted_iota(jnp.int32, (group, group), 0)
    column = lax.broadcasted_iota(jnp.int32, (group, group), 1)
    kind = column // kept
    column = column % kept
    chip = (column // slot_rows + TURN_Y) % (kept // slot_rows)
    place = chip * pair + (column + turn) % slot_rows + (kind ^ core) * slot_rows
    pick = jnp.where(row == place, 1.0, 0.0).astype(BF16)
    for load, rows in zip(loads, chunks):
        load.wait()
        blocks = q.shape[1] // group
        for b in range(blocks):
            picked = dot(q[rows, b * group : (b + 1) * group], pick).astype(BF16)
            place = (b - TURN_X) % blocks
            columns = slice(place * kept, (place + 1) * kept)
            own_q[rows, columns] = picked[:, :kept]
            other_q[rows, columns] = picked[:, kept:]
    loads[CHUNKS].wait()
    logits[...] = dot(x[...], own_q[...])


def column_kernel(own_q, x, x2, logits, out):
    width = own_q.shape[0]
    second = dot(x2[...], own_q[...])
    first = logits[...]
    top1 = peak_of(first)
    first = jnp.exp(first - top1)
    total1 = jnp.sum(first, axis=0, keepdims=True)
    sums1 = dot(first.astype(BF16), x[...], OVER_ROWS)
    top2 = peak_of(second)
    second = jnp.exp(second - top2)
    total2 = jnp.sum(second, axis=0, keepdims=True)
    sums2 = dot(second.astype(BF16), x2[...], OVER_ROWS)
    top = jnp.maximum(top1, top2)
    w1, w2 = jnp.exp(top1 - top), jnp.exp(top2 - top)
    total = total1 * w1 + total2 * w2
    high = total.astype(BF16).astype(F32)
    kind = lax.broadcasted_iota(jnp.int32, (LANES, top.shape[1]), 0)
    stats = total - high
    for place, value in enumerate((top, high, w1, w2)):
        stats = jnp.where(kind == place, value, stats)
    columns = stats.T
    sums = (sums1 * columns[:, 2:3] + sums2 * columns[:, 3:4]).astype(BF16)
    stats = stats[:TAIL].astype(BF16)
    chips, rows, _ = out.shape
    held = top.shape[1] // chips
    for c in range(chips):
        for j in range(width // LANES):
            part = slice(j * LANES, (j + 1) * LANES)
            out[c, j * held : (j + 1) * held, :] = sums[c * held : (c + 1) * held, part]
        group = c * held // LANES * LANES
        out[c, rows - TAIL :, :] = stats[:, group : group + LANES]


def softmax_kernel(x, other_q, logits, own_w, other_w):
    own = logits[...]
    other = dot(x[...], other_q[...])
    top = jnp.maximum(jnp.max(own, axis=1, keepdims=True), jnp.max(other, axis=1, keepdims=True))
    own = jnp.exp(own - top)
    other = jnp.exp(other - top)
    total = jnp.sum(own, axis=1, keepdims=True) + jnp.sum(other, axis=1, keepdims=True)
    scale = 1.0 / total
    own_w[...] = (own * scale).astype(BF16)
    other_w[...] = (other * scale).astype(BF16)


def combine_kernel(parts, out, weights, scratch):
    chips, rows, _ = parts.shape
    groups, size, width = out.shape
    held = groups * size
    source = lax.broadcasted_iota(jnp.int32, (LANES, LANES), 0)
    top = jnp.full((LANES, LANES), -jnp.inf, F32)
    total = jnp.zeros((LANES, LANES), F32)
    for c in range(chips):
        stats = parts[c, rows - TAIL :, :].astype(F32)
        top = jnp.where(source == c, stats[0:1], top)
        total = jnp.where(source == c, stats[1:2] + stats[4:5], total)
    weight = jnp.exp(top - jnp.max(top, axis=0, keepdims=True))
    weight = weight / jnp.sum(total * weight, axis=0, keepdims=True)
    weights[...] = weight.T
    place = (lax.axis_index("y") - TURN_Y) % (LANES // held)
    start = pl.multiple_of(place * held, held)
    mine = weights[pl.ds(start, held), :]
    for j in range(width // LANES):
        part = slice(j * LANES, (j + 1) * LANES)
        acc = jnp.zeros((held, LANES), F32)
        for c in range(chips):
            acc = acc + mine[:, c : c + 1] * parts[c, j * held : (j + 1) * held, :].astype(F32)
        scratch[:, part] = acc
    for g in range(groups):
        out[g] = scratch[g * size : (g + 1) * size, :].astype(BF16)


def expert_kernel(received, w_in, w_out, out, scratch):
    groups, held, _ = received.shape
    for g in range(groups):
        scratch[g * held : (g + 1) * held, :] = received[g].astype(F32)
    x = scratch[...].astype(BF16)
    h = jax.nn.gelu(dot(x, w_in[...]), approximate=True).astype(BF16)
    scratch[...] = dot(h, w_out[...])
    for g in range(groups):
        out[g] = scratch[g * held : (g + 1) * held, :].astype(BF16)


def final_kernel(partial, weights, rows, out, buffer, sems):
    count = buffer.shape[0] // PIECES
    stores = []
    for i in range(PIECES):
        part = slice(i * count, (i + 1) * count)
        buffer[part, :] = (partial[part, :] + dot(weights[part, :], rows[...])).astype(BF16)
        stores.append(pltpu.make_async_copy(buffer.at[part, :], out.at[part, :], sems.at[i]))
        stores[i].start()
    for store in stores:
        store.wait()


def turned(size, turn):
    return [(i + turn) % size for i in range(size)]


def plane_groups(by_row=False):
    xs, ys = turned(lax.axis_size("x"), TURN_X), turned(lax.axis_size("y"), TURN_Y)
    order = [(x, y) for y in ys for x in xs] if by_row else [(x, y) for x in xs for y in ys]
    return [[(x * len(ys) + y) * 2 + core for x, y in order] for core in range(2)]


def exchange(values, axes, groups):
    return lax.all_to_all(
        values, axes, split_axis=0, concat_axis=0, tiled=True, axis_index_groups=groups
    )


def per_device(tokens, slot_query, expert_in, expert_out):
    x = tokens[0]
    count, width = x.shape
    chips = lax.axis_size("x") * lax.axis_size("y")
    grp_count = lax.axis_size("grp")
    slots = slot_query.shape[1]
    half = slots // 2
    slot_rows = half // chips
    x2 = lax.ppermute(x, "core", SWAP)
    shape = jax.ShapeDtypeStruct
    own_q, other_q, kept, logits = call(
        functools.partial(logit_kernel, slot_rows, slot_rows // grp_count * TURN_Z),
        [
            shape((width, half), BF16),
            shape((width, half), BF16),
            shape((count, width), BF16),
            shape((count, half), F32),
        ],
        2 * slots * width * count, 5_000_000,
        [pltpu.with_memory_space_constraint(a, pltpu.HBM) for a in (slot_query, x)],
        [pltpu.VMEM((width, slots), BF16), pltpu.SemaphoreType.DMA((CHUNKS + 1,))],
        pl.ANY,
    )
    (packed,) = call(
        column_kernel,
        [shape((chips, slot_rows * width // LANES + TAIL, LANES), BF16)],
        3 * slots * width * count, 5_000_000, (own_q, kept, x2, logits),
    )
    w_in, w_out = expert_in[0], expert_out[0]
    parts = exchange(packed, CTX, plane_groups())
    block = shape((grp_count, slot_rows // grp_count, width), BF16)
    rows = [pltpu.VMEM((slot_rows, width), F32)]
    (slot_inputs,) = call(
        combine_kernel, [block], 2 * half * width, 1_000_000, (parts,),
        [pltpu.VMEM((LANES, LANES), F32)] + rows,
    )
    line = [turned(grp_count, TURN_Z)]
    received = exchange(slot_inputs, "grp", line)
    (produced,) = call(
        expert_kernel,
        [block],
        4 * slot_rows * width * expert_in.shape[2], 9_500_000,
        (
            received,
            pltpu.with_memory_space_constraint(w_in, pltpu.VMEM),
            pltpu.with_memory_space_constraint(w_out, pltpu.VMEM),
        ),
        rows,
    )
    returned = exchange(produced, "grp", line).reshape(1, slot_rows, width)
    copies = jnp.broadcast_to(returned, (chips, slot_rows, width))
    own = exchange(copies, CTX, plane_groups()).reshape(half, width)
    other = lax.ppermute(own, "core", SWAP)
    own_w, other_w = call(
        softmax_kernel,
        [shape((count, half), BF16), shape((count, half), BF16)],
        slots * width * count, 4_000_000, (kept, other_q, logits),
    )
    (mixed,) = call(
        final_kernel,
        [shape((count, width), BF16)],
        slots * width * count, 4_000_000, (dot(own_w, own), other_w, other),
        [pltpu.VMEM((count, width), BF16), pltpu.SemaphoreType.DMA((PIECES,))],
        to=pl.ANY,
    )
    return mixed[None]


def solution(mesh):
    fine = Mesh(mesh.devices.reshape(4, 4, 2, 8), ("x", "y", "core", "grp"))
    in_specs = (
        P("grp", CTX, None),
        P(),
        P(CTX + ("grp",), None, None),
        P(CTX + ("grp",), None, None),
    )
    return jax.shard_map(
        per_device, mesh=fine, in_specs=in_specs, out_specs=P("grp", CTX, None), check_vma=False
    )
```

```python
import functools

import jax
import jax.numpy as jnp
from jax import lax
from jax.experimental import pallas as pl
from jax.experimental.pallas import tpu as pltpu
from jax.sharding import Mesh, PartitionSpec as P

BF16 = jnp.bfloat16
F32 = jnp.float32
SWAP = [(0, 1), (1, 0)]
CTX = ("x", "y", "core")
LIMIT = 24 * 1024 * 1024
LANES = 128
TAIL = 16
CHUNKS = 2
PIECES = 4
TURN_X, TURN_Y, TURN_Z = 2, 2, 4
OVER_ROWS = (((0,), (0,)), ((), ()))


def dot(a, b, dims=(((1,), (0,)), ((), ()))):
    return lax.dot_general(a, b, dims, preferred_element_type=F32)


def call(body, outs, flops, moved, args, scratch=(), space=pltpu.VMEM, to=pltpu.VMEM):
    return pl.pallas_call(
        body,
        out_shape=outs,
        in_specs=[pl.BlockSpec(memory_space=space)] * len(args),
        out_specs=[pl.BlockSpec(memory_space=to)] * len(outs),
        scratch_shapes=list(scratch),
        compiler_params=pltpu.CompilerParams(vmem_limit_bytes=LIMIT),
        cost_estimate=pl.CostEstimate(flops=flops, bytes_accessed=moved, transcendentals=0),
    )(*args)


def peak_of(logits):
    return jnp.max(logits, axis=0, keepdims=True).astype(BF16).astype(F32)


def logit_kernel(slot_rows, turn, q_hbm, x_hbm, own_q, q, pick_other, x, logits, sems):
    group = 256
    kept = group // 2
    chunk = q.shape[0] // CHUNKS
    chunks = [slice(i * chunk, (i + 1) * chunk) for i in range(CHUNKS)]
    loads = [
        pltpu.make_async_copy(q_hbm.at[rows, :], q.at[rows, :], sems.at[i])
        for i, rows in enumerate(chunks)
    ]
    loads.append(pltpu.make_async_copy(x_hbm, x, sems.at[CHUNKS]))
    for load in loads:
        load.start()
    core = lax.axis_index("core")
    pair = 2 * slot_rows
    row = lax.broadcasted_iota(jnp.int32, (group, group), 0)
    column = lax.broadcasted_iota(jnp.int32, (group, group), 1)
    kind = column // kept
    column = column % kept
    chip = (column // slot_rows + TURN_Y) % (kept // slot_rows)
    place = chip * pair + (column + turn) % slot_rows + (kind ^ core) * slot_rows
    pick = jnp.where(row == place, 1.0, 0.0).astype(BF16)
    pick_other[...] = pick[:, kept:]
    for load, rows in zip(loads, chunks):
        load.wait()
        blocks = q.shape[1] // group
        for b in range(blocks):
            picked = dot(q[rows, b * group : (b + 1) * group], pick[:, :kept]).astype(BF16)
            place = (b - TURN_X) % blocks
            columns = slice(place * kept, (place + 1) * kept)
            own_q[rows, columns] = picked
    loads[CHUNKS].wait()
    logits[...] = dot(x[...], own_q[...])


def column_kernel(own_q, x, x2, logits, out):
    width = own_q.shape[0]
    second = dot(x2[...], own_q[...])
    first = logits[...]
    top1 = peak_of(first)
    first = jnp.exp(first - top1)
    total1 = jnp.sum(first, axis=0, keepdims=True)
    sums1 = dot(first.astype(BF16), x[...], OVER_ROWS)
    top2 = peak_of(second)
    second = jnp.exp(second - top2)
    total2 = jnp.sum(second, axis=0, keepdims=True)
    sums2 = dot(second.astype(BF16), x2[...], OVER_ROWS)
    top = jnp.maximum(top1, top2)
    w1, w2 = jnp.exp(top1 - top), jnp.exp(top2 - top)
    total = total1 * w1 + total2 * w2
    high = total.astype(BF16).astype(F32)
    kind = lax.broadcasted_iota(jnp.int32, (LANES, top.shape[1]), 0)
    stats = total - high
    for place, value in enumerate((top, high, w1, w2)):
        stats = jnp.where(kind == place, value, stats)
    columns = stats.T
    sums = (sums1 * columns[:, 2:3] + sums2 * columns[:, 3:4]).astype(BF16)
    stats = stats[:TAIL].astype(BF16)
    chips, rows, _ = out.shape
    held = top.shape[1] // chips
    for c in range(chips):
        for j in range(width // LANES):
            part = slice(j * LANES, (j + 1) * LANES)
            out[c, j * held : (j + 1) * held, :] = sums[c * held : (c + 1) * held, part]
        group = c * held // LANES * LANES
        out[c, rows - TAIL :, :] = stats[:, group : group + LANES]


def softmax_kernel(x, q, pick, logits, own_w, other_w):
    own = logits[...]
    group, kept = pick.shape
    blocks = q.shape[1] // group
    parts = []
    for place in range(blocks):
        b = (place + TURN_X) % blocks
        parts.append(dot(q[:, b * group : (b + 1) * group], pick[...]).astype(BF16))
    other = dot(x[...], jnp.concatenate(parts, axis=1))
    top = jnp.maximum(jnp.max(own, axis=1, keepdims=True), jnp.max(other, axis=1, keepdims=True))
    own = jnp.exp(own - top)
    other = jnp.exp(other - top)
    total = jnp.sum(own, axis=1, keepdims=True) + jnp.sum(other, axis=1, keepdims=True)
    scale = 1.0 / total
    own_w[...] = (own * scale).astype(BF16)
    other_w[...] = (other * scale).astype(BF16)


def combine_kernel(parts, out, weights, scratch):
    chips, rows, _ = parts.shape
    groups, size, width = out.shape
    held = groups * size
    source = lax.broadcasted_iota(jnp.int32, (LANES, LANES), 0)
    top = jnp.full((LANES, LANES), -jnp.inf, F32)
    total = jnp.zeros((LANES, LANES), F32)
    for c in range(chips):
        stats = parts[c, rows - TAIL :, :].astype(F32)
        top = jnp.where(source == c, stats[0:1], top)
        total = jnp.where(source == c, stats[1:2] + stats[4:5], total)
    weight = jnp.exp(top - jnp.max(top, axis=0, keepdims=True))
    weight = weight / jnp.sum(total * weight, axis=0, keepdims=True)
    weights[...] = weight.T
    place = (lax.axis_index("y") - TURN_Y) % (LANES // held)
    start = pl.multiple_of(place * held, held)
    mine = weights[pl.ds(start, held), :]
    for j in range(width // LANES):
        part = slice(j * LANES, (j + 1) * LANES)
        acc = jnp.zeros((held, LANES), F32)
        for c in range(chips):
            acc = acc + mine[:, c : c + 1] * parts[c, j * held : (j + 1) * held, :].astype(F32)
        scratch[:, part] = acc
    for g in range(groups):
        out[g] = scratch[g * size : (g + 1) * size, :].astype(BF16)


def expert_kernel(received, w_in, w_out, out, scratch):
    groups, held, _ = received.shape
    for g in range(groups):
        scratch[g * held : (g + 1) * held, :] = received[g].astype(F32)
    x = scratch[...].astype(BF16)
    h = jax.nn.gelu(dot(x, w_in[...]), approximate=True).astype(BF16)
    scratch[...] = dot(h, w_out[...])
    for g in range(groups):
        out[g] = scratch[g * held : (g + 1) * held, :].astype(BF16)


def final_kernel(partial, weights, rows, out, buffer, sems):
    count = buffer.shape[0] // PIECES
    stores = []
    for i in range(PIECES):
        part = slice(i * count, (i + 1) * count)
        buffer[part, :] = (partial[part, :] + dot(weights[part, :], rows[...])).astype(BF16)
        stores.append(pltpu.make_async_copy(buffer.at[part, :], out.at[part, :], sems.at[i]))
        stores[i].start()
    for store in stores:
        store.wait()


def turned(size, turn):
    return [(i + turn) % size for i in range(size)]


def plane_groups(by_row=False):
    xs, ys = turned(lax.axis_size("x"), TURN_X), turned(lax.axis_size("y"), TURN_Y)
    order = [(x, y) for y in ys for x in xs] if by_row else [(x, y) for x in xs for y in ys]
    return [[(x * len(ys) + y) * 2 + core for x, y in order] for core in range(2)]


def exchange(values, axes, groups):
    return lax.all_to_all(
        values, axes, split_axis=0, concat_axis=0, tiled=True, axis_index_groups=groups
    )


def per_device(tokens, slot_query, expert_in, expert_out):
    x = tokens[0]
    count, width = x.shape
    chips = lax.axis_size("x") * lax.axis_size("y")
    grp_count = lax.axis_size("grp")
    slots = slot_query.shape[1]
    half = slots // 2
    slot_rows = half // chips
    x2 = lax.ppermute(x, "core", SWAP)
    shape = jax.ShapeDtypeStruct
    own_q, query, pick, kept, logits = call(
        functools.partial(logit_kernel, slot_rows, slot_rows // grp_count * TURN_Z),
        [
            shape((width, half), BF16),
            shape((width, slots), BF16),
            shape((2 * LANES, LANES), BF16),
            shape((count, width), BF16),
            shape((count, half), F32),
        ],
        2 * slots * width * count, 5_000_000,
        [pltpu.with_memory_space_constraint(a, pltpu.HBM) for a in (slot_query, x)],
        [pltpu.SemaphoreType.DMA((CHUNKS + 1,))],
        pl.ANY,
    )
    (packed,) = call(
        column_kernel,
        [shape((chips, slot_rows * width // LANES + TAIL, LANES), BF16)],
        3 * slots * width * count, 5_000_000, (own_q, kept, x2, logits),
    )
    w_in, w_out = expert_in[0], expert_out[0]
    parts = exchange(packed, CTX, plane_groups())
    block = shape((grp_count, slot_rows // grp_count, width), BF16)
    rows = [pltpu.VMEM((slot_rows, width), F32)]
    (slot_inputs,) = call(
        combine_kernel, [block], 2 * half * width, 1_000_000, (parts,),
        [pltpu.VMEM((LANES, LANES), F32)] + rows,
    )
    line = [turned(grp_count, TURN_Z)]
    received = exchange(slot_inputs, "grp", line)
    (produced,) = call(
        expert_kernel,
        [block],
        4 * slot_rows * width * expert_in.shape[2], 9_500_000,
        (
            received,
            pltpu.with_memory_space_constraint(w_in, pltpu.VMEM),
            pltpu.with_memory_space_constraint(w_out, pltpu.VMEM),
        ),
        rows,
    )
    returned = exchange(produced, "grp", line).reshape(1, slot_rows, width)
    copies = jnp.broadcast_to(returned, (chips, slot_rows, width))
    own = exchange(copies, CTX, plane_groups()).reshape(half, width)
    other = lax.ppermute(own, "core", SWAP)
    own_w, other_w = call(
        softmax_kernel,
        [shape((count, half), BF16), shape((count, half), BF16)],
        slots * width * count, 4_000_000, (kept, query, pick, logits),
    )
    (mixed,) = call(
        final_kernel,
        [shape((count, width), BF16)],
        slots * width * count, 4_000_000, (dot(own_w, own), other_w, other),
        [pltpu.VMEM((count, width), BF16), pltpu.SemaphoreType.DMA((PIECES,))],
        to=pl.ANY,
    )
    return mixed[None]


def solution(mesh):
    fine = Mesh(mesh.devices.reshape(4, 4, 2, 8), ("x", "y", "core", "grp"))
    in_specs = (
        P("grp", CTX, None),
        P(),
        P(CTX + ("grp",), None, None),
        P(CTX + ("grp",), None, None),
    )
    return jax.shard_map(
        per_device, mesh=fine, in_specs=in_specs, out_specs=P("grp", CTX, None), check_vma=False
    )
```

```python
import functools

import jax
import jax.numpy as jnp
from jax import lax
from jax.experimental import pallas as pl
from jax.experimental.pallas import tpu as pltpu
from jax.sharding import Mesh, PartitionSpec as P

BF16 = jnp.bfloat16
F32 = jnp.float32
SWAP = [(0, 1), (1, 0)]
CTX = ("x", "y", "core")
LIMIT = 24 * 1024 * 1024
LANES = 128
TAIL = 16
CHUNKS = 2
PIECES = 4
TURN_X, TURN_Y, TURN_Z = 2, 2, 5
OVER_ROWS = (((0,), (0,)), ((), ()))


def dot(a, b, dims=(((1,), (0,)), ((), ()))):
    return lax.dot_general(a, b, dims, preferred_element_type=F32)


def call(body, outs, flops, moved, args, scratch=(), space=pltpu.VMEM, to=pltpu.VMEM):
    return pl.pallas_call(
        body,
        out_shape=outs,
        in_specs=[pl.BlockSpec(memory_space=space)] * len(args),
        out_specs=[pl.BlockSpec(memory_space=to)] * len(outs),
        scratch_shapes=list(scratch),
        compiler_params=pltpu.CompilerParams(vmem_limit_bytes=LIMIT),
        cost_estimate=pl.CostEstimate(flops=flops, bytes_accessed=moved, transcendentals=0),
    )(*args)


def peak_of(logits):
    return jnp.max(logits, axis=0, keepdims=True).astype(BF16).astype(F32)


def logit_kernel(slot_rows, turn, q_hbm, x_hbm, own_q, other_q, x, logits, q, sems):
    group = 256
    kept = group // 2
    chunk = q.shape[0] // CHUNKS
    chunks = [slice(i * chunk, (i + 1) * chunk) for i in range(CHUNKS)]
    loads = [
        pltpu.make_async_copy(q_hbm.at[rows, :], q.at[rows, :], sems.at[i])
        for i, rows in enumerate(chunks)
    ]
    loads.append(pltpu.make_async_copy(x_hbm, x, sems.at[CHUNKS]))
    for load in loads:
        load.start()
    core = lax.axis_index("core")
    pair = 2 * slot_rows
    row = lax.broadcasted_iota(jnp.int32, (group, group), 0)
    column = lax.broadcasted_iota(jnp.int32, (group, group), 1)
    kind = column // kept
    column = column % kept
    chip = (column // slot_rows + TURN_Y) % (kept // slot_rows)
    place = chip * pair + (column + turn) % slot_rows + (kind ^ core) * slot_rows
    pick = jnp.where(row == place, 1.0, 0.0).astype(BF16)
    for load, rows in zip(loads, chunks):
        load.wait()
        blocks = q.shape[1] // group
        for b in range(blocks):
            picked = dot(q[rows, b * group : (b + 1) * group], pick).astype(BF16)
            place = (b - TURN_X) % blocks
            columns = slice(place * kept, (place + 1) * kept)
            own_q[rows, columns] = picked[:, :kept]
            other_q[rows, columns] = picked[:, kept:]
    loads[CHUNKS].wait()
    logits[...] = dot(x[...], own_q[...])


def column_kernel(own_q, x, x2, logits, out):
    width = own_q.shape[0]
    second = dot(x2[...], own_q[...])
    first = logits[...]
    top1 = peak_of(first)
    first = jnp.exp(first - top1)
    total1 = jnp.sum(first, axis=0, keepdims=True)
    sums1 = dot(first.astype(BF16), x[...], OVER_ROWS)
    top2 = peak_of(second)
    second = jnp.exp(second - top2)
    total2 = jnp.sum(second, axis=0, keepdims=True)
    sums2 = dot(second.astype(BF16), x2[...], OVER_ROWS)
    top = jnp.maximum(top1, top2)
    w1, w2 = jnp.exp(top1 - top), jnp.exp(top2 - top)
    total = total1 * w1 + total2 * w2
    high = total.astype(BF16).astype(F32)
    kind = lax.broadcasted_iota(jnp.int32, (LANES, top.shape[1]), 0)
    stats = total - high
    for place, value in enumerate((top, high, w1, w2)):
        stats = jnp.where(kind == place, value, stats)
    columns = stats.T
    sums = (sums1 * columns[:, 2:3] + sums2 * columns[:, 3:4]).astype(BF16)
    stats = stats[:TAIL].astype(BF16)
    chips, rows, _ = out.shape
    held = top.shape[1] // chips
    for c in range(chips):
        for j in range(width // LANES):
            part = slice(j * LANES, (j + 1) * LANES)
            out[c, j * held : (j + 1) * held, :] = sums[c * held : (c + 1) * held, part]
        group = c * held // LANES * LANES
        out[c, rows - TAIL :, :] = stats[:, group : group + LANES]


def softmax_kernel(x, other_q, logits, own_w, other_w):
    own = logits[...]
    other = dot(x[...], other_q[...])
    top = jnp.maximum(jnp.max(own, axis=1, keepdims=True), jnp.max(other, axis=1, keepdims=True))
    own = jnp.exp(own - top)
    other = jnp.exp(other - top)
    total = jnp.sum(own, axis=1, keepdims=True) + jnp.sum(other, axis=1, keepdims=True)
    scale = 1.0 / total
    own_w[...] = (own * scale).astype(BF16)
    other_w[...] = (other * scale).astype(BF16)


def combine_kernel(parts, out, weights, scratch):
    chips, rows, _ = parts.shape
    groups, size, width = out.shape
    held = groups * size
    source = lax.broadcasted_iota(jnp.int32, (LANES, LANES), 0)
    top = jnp.full((LANES, LANES), -jnp.inf, F32)
    total = jnp.zeros((LANES, LANES), F32)
    for c in range(chips):
        stats = parts[c, rows - TAIL :, :].astype(F32)
        top = jnp.where(source == c, stats[0:1], top)
        total = jnp.where(source == c, stats[1:2] + stats[4:5], total)
    weight = jnp.exp(top - jnp.max(top, axis=0, keepdims=True))
    weight = weight / jnp.sum(total * weight, axis=0, keepdims=True)
    weights[...] = weight.T
    place = (lax.axis_index("y") - TURN_Y) % (LANES // held)
    start = pl.multiple_of(place * held, held)
    mine = weights[pl.ds(start, held), :]
    for j in range(width // LANES):
        part = slice(j * LANES, (j + 1) * LANES)
        acc = jnp.zeros((held, LANES), F32)
        for c in range(chips):
            acc = acc + mine[:, c : c + 1] * parts[c, j * held : (j + 1) * held, :].astype(F32)
        scratch[:, part] = acc
    for g in range(groups):
        out[g] = scratch[g * size : (g + 1) * size, :].astype(BF16)


def expert_kernel(received, w_in, w_out, out, scratch):
    groups, held, _ = received.shape
    for g in range(groups):
        scratch[g * held : (g + 1) * held, :] = received[g].astype(F32)
    x = scratch[...].astype(BF16)
    h = jax.nn.gelu(dot(x, w_in[...]), approximate=True).astype(BF16)
    scratch[...] = dot(h, w_out[...])
    for g in range(groups):
        out[g] = scratch[g * held : (g + 1) * held, :].astype(BF16)


def final_kernel(partial, weights, rows, out, buffer, sems):
    count = buffer.shape[0] // PIECES
    stores = []
    for i in range(PIECES):
        part = slice(i * count, (i + 1) * count)
        buffer[part, :] = (partial[part, :] + dot(weights[part, :], rows[...])).astype(BF16)
        stores.append(pltpu.make_async_copy(buffer.at[part, :], out.at[part, :], sems.at[i]))
        stores[i].start()
    for store in stores:
        store.wait()


def turned(size, turn):
    return [(i + turn) % size for i in range(size)]


def plane_groups(by_row=False):
    xs, ys = turned(lax.axis_size("x"), TURN_X), turned(lax.axis_size("y"), TURN_Y)
    order = [(x, y) for y in ys for x in xs] if by_row else [(x, y) for x in xs for y in ys]
    return [[(x * len(ys) + y) * 2 + core for x, y in order] for core in range(2)]


def exchange(values, axes, groups):
    return lax.all_to_all(
        values, axes, split_axis=0, concat_axis=0, tiled=True, axis_index_groups=groups
    )


def per_device(tokens, slot_query, expert_in, expert_out):
    x = tokens[0]
    count, width = x.shape
    chips = lax.axis_size("x") * lax.axis_size("y")
    grp_count = lax.axis_size("grp")
    slots = slot_query.shape[1]
    half = slots // 2
    slot_rows = half // chips
    x2 = lax.ppermute(x, "core", SWAP)
    shape = jax.ShapeDtypeStruct
    own_q, other_q, kept, logits = call(
        functools.partial(logit_kernel, slot_rows, slot_rows // grp_count * TURN_Z),
        [
            shape((width, half), BF16),
            shape((width, half), BF16),
            shape((count, width), BF16),
            shape((count, half), F32),
        ],
        2 * slots * width * count, 5_000_000,
        [pltpu.with_memory_space_constraint(a, pltpu.HBM) for a in (slot_query, x)],
        [pltpu.VMEM((width, slots), BF16), pltpu.SemaphoreType.DMA((CHUNKS + 1,))],
        pl.ANY,
    )
    (packed,) = call(
        column_kernel,
        [shape((chips, slot_rows * width // LANES + TAIL, LANES), BF16)],
        3 * slots * width * count, 5_000_000, (own_q, kept, x2, logits),
    )
    w_in, w_out = expert_in[0], expert_out[0]
    parts = exchange(packed, CTX, plane_groups())
    block = shape((grp_count, slot_rows // grp_count, width), BF16)
    rows = [pltpu.VMEM((slot_rows, width), F32)]
    (slot_inputs,) = call(
        combine_kernel, [block], 2 * half * width, 1_000_000, (parts,),
        [pltpu.VMEM((LANES, LANES), F32)] + rows,
    )
    line = [turned(grp_count, TURN_Z)]
    received = exchange(slot_inputs, "grp", line)
    (produced,) = call(
        expert_kernel,
        [block],
        4 * slot_rows * width * expert_in.shape[2], 9_500_000,
        (
            received,
            pltpu.with_memory_space_constraint(w_in, pltpu.VMEM),
            pltpu.with_memory_space_constraint(w_out, pltpu.VMEM),
        ),
        rows,
    )
    returned = exchange(produced, "grp", line).reshape(1, slot_rows, width)
    copies = jnp.broadcast_to(returned, (chips, slot_rows, width))
    own = exchange(copies, CTX, plane_groups()).reshape(half, width)
    other = lax.ppermute(own, "core", SWAP)
    own_w, other_w = call(
        softmax_kernel,
        [shape((count, half), BF16), shape((count, half), BF16)],
        slots * width * count, 4_000_000, (kept, other_q, logits),
    )
    (mixed,) = call(
        final_kernel,
        [shape((count, width), BF16)],
        slots * width * count, 4_000_000, (dot(own_w, own), other_w, other),
        [pltpu.VMEM((count, width), BF16), pltpu.SemaphoreType.DMA((PIECES,))],
        to=pl.ANY,
    )
    return mixed[None]


def solution(mesh):
    fine = Mesh(mesh.devices.reshape(4, 4, 2, 8), ("x", "y", "core", "grp"))
    in_specs = (
        P("grp", CTX, None),
        P(),
        P(CTX + ("grp",), None, None),
        P(CTX + ("grp",), None, None),
    )
    return jax.shard_map(
        per_device, mesh=fine, in_specs=in_specs, out_specs=P("grp", CTX, None), check_vma=False
    )
```
